256 devices in a mesh: dom: 32 (over x, y, core), sub: 8 (over z).
Axes of the slice: x: 4, y: 4, z: 8, core: 2. Of those that a mesh axis runs over, the one named last changes fastest.
Arguments:
- a_tiles: bfloat16 [4096, 4, 128, 128], P(('dom', 'sub')), may hold values from -0.25 to 0.25
- columns: int32 [4096, 4], P(('dom', 'sub')), may hold values from 0 to 4095, as said below
- aggregate: int32 [4096], P(('dom', 'sub')), may hold values from 0 to 511, as said below
- tentative: bfloat16 [4096, 128, 128], P(('dom', 'sub')), may hold values from -0.75 to 0.75
- inverse_diag: bfloat16 [4096, 128, 128], P(('dom', 'sub')), may hold values from -0.5 to 0.5
Outputs:
- coarse: float32 [512, 7, 128, 128], P('dom', None, 'sub')
The draws below stay inside these ranges and needn't reach their ends.
Inputs may be any that keep to these rules, and one draw needn't show every extreme that they name: Ids never fall along the block rows; every aggregate is a run of block rows of one device and each device's first block row begins one. Index d of dom holds exactly the aggregates d * 16 to (d + 1) * 16 - 1. A device holds at most 3 aggregates, and some device of every index of dom holds exactly 3. columns[i, 0] is i; every column j of row i has aggregate[j] within one of aggregate[i]; columns may repeat.
All inputs are finite; a program needn't handle non-finite values.
Results may differ from the reference program's by a relative error of at most 0.0055.
Values may be sent and summed in bfloat16 or wider, within the bound.
No kernel may reach another device: no remote copies, remote signals or barrier semaphores. Data moves between devices by JAX's collectives and lax.ppermute only.
A program may use at most 64 MiB of HBM per device.

```python
import jax
import jax.numpy as jnp
from jax import lax

B = 128
AGG_DEV = 2
K = 4
FR_DEV = 16
WIN = 5
CR_DOM = 16
NF = 4096
NC = 512


def shuffled(key_one):
    return jax.random.permutation(key_one, FR_DEV - 1)


def layout(key):
    devices_total = NF // FR_DEV
    sub_count = CR_DOM // AGG_DEV
    parts = devices_total // sub_count
    pairs = sub_count // 2
    key_delta, key_sign, key_cut = jax.random.split(jax.random.fold_in(key, 101), 3)
    delta = jax.random.randint(key_delta, (parts, pairs), 0, AGG_DEV)
    delta = delta.at[:, 0].set(AGG_DEV - 1)
    signs = jax.random.randint(key_sign, (parts, pairs), 0, 2) * 2 - 1
    counts = jnp.stack([AGG_DEV + signs * delta, AGG_DEV - signs * delta], axis=-1).reshape(devices_total)
    orders = jax.vmap(shuffled)(jax.random.split(key_cut, devices_total))
    cuts = (orders < (counts - 1)[:, None]).astype(jnp.int32)
    local = jnp.concatenate([jnp.zeros((devices_total, 1), jnp.int32), jnp.cumsum(cuts, axis=1)], axis=1)
    begins = jnp.cumsum(counts) - counts
    return (begins[:, None] + local).reshape(NF).astype(jnp.int32)


def draw_aggregate(key, part):
    aggregate = layout(key)
    return aggregate


def draw_columns(key, part):
    aggregate = layout(key)
    key = jax.random.fold_in(key, 7)
    lowest = jnp.searchsorted(aggregate, aggregate - 1, side='left').astype(jnp.int32)
    highest = jnp.searchsorted(aggregate, aggregate + 2, side='left').astype(jnp.int32)
    spread_rows = highest - lowest
    picks = jax.random.randint(key, (NF, K), 0, 1 << 20)
    columns = lowest[:, None] + picks % spread_rows[:, None]
    columns = columns.at[:, 0].set(jnp.arange(NF, dtype=jnp.int32))
    return columns.astype(jnp.int32)


def level_of(stream_key, dims, shards, least, largest):
    level = 1.0
    for axis_at, blocks in shards:
        draws = jax.random.uniform(jax.random.fold_in(jax.random.fold_in(stream_key, 6), axis_at), (blocks,), jnp.float32, least / len(shards), largest / len(shards))
        level = level * jnp.repeat(jnp.exp(draws), dims[axis_at] // blocks).reshape((-1,) + (1,) * (len(dims) - 1 - axis_at))
    return level


def scatter_about(stream_key, extent, deviation, most, cuts=(), kind=jnp.bfloat16):
    drawn = jax.random.normal(stream_key, extent, jnp.float32) * deviation
    if len(cuts) > 0:
        drawn = level_of(stream_key, extent, cuts, -0.22, 0.18) * drawn
    return jnp.clip(drawn, min=-most, max=most).astype(kind)


def setup_inputs(seed: int = 0) -> dict:
    key_of = jax.random.split(jax.random.key(seed), 6)
    return {
        "a_tiles": scatter_about(key_of[0], (NF, K, B, B), (B * K) ** -0.5, 0.25, ((0, 256),)),
        "columns": draw_columns(jax.random.fold_in(key_of[5], 71), 0),
        "aggregate": draw_aggregate(jax.random.fold_in(key_of[5], 71), 0),
        "tentative": scatter_about(key_of[3], (NF, B, B), 0.125, 0.75, ((0, 256),)),
        "inverse_diag": scatter_about(key_of[4], (NF, B, B), B ** -0.5, 0.5, ((0, 256),)),
    }


OMEGA = 0.6


def neighbour_sum(a_tiles, picked, offsets):
    sources = picked.shape[2]
    band_list = []
    for target in range(sources + 2):
        chosen = jnp.zeros_like(picked[:, :, 0])
        for source in range(sources):
            matches = (offsets + 1 + source == target)[:, :, None, None]
            chosen = jnp.where(matches, picked[:, :, source], chosen)
        band_list.append(jnp.einsum("ikab,ikbc->iac", a_tiles.astype(jnp.float32), chosen.astype(jnp.float32), precision=lax.Precision.HIGHEST))
    return jnp.stack(band_list, axis=1)


def window_sum(smooth, product, relative, window_rows):
    tile_order = smooth.shape[-1]
    window_slots = jnp.arange(window_rows, dtype=jnp.int32)
    band_list = [jnp.zeros((window_rows, tile_order, tile_order), jnp.float32) for unused in range(7)]
    for source in range(3):
        placing = ((relative + source)[:, None] == window_slots[None, :]).astype(jnp.float32)
        for target in range(5):
            partial_tile = jnp.einsum("iba,ibc->iac", smooth[:, source].astype(jnp.float32), product[:, target].astype(jnp.float32), precision=lax.Precision.HIGHEST)
            band_list[target - source + 2] = band_list[target - source + 2] + jnp.einsum("ir,iac->rac", placing, partial_tile, precision=lax.Precision.HIGHEST)
    return jnp.stack(band_list, axis=1)


def reference(a_tiles, columns, aggregate, tentative, inverse_diag):
    total_rows = a_tiles.shape[0]
    blocks = total_rows // FR_DEV
    tile_order = a_tiles.shape[-1]
    offsets_all = (aggregate[columns] - aggregate[:, None]).astype(jnp.int32)
    centre = (jnp.arange(3) == 1).astype(jnp.float32)[None, :, None, None]

    def smooth_block(index):
        begin = (index * FR_DEV).astype(jnp.int32)
        a_block = lax.dynamic_slice_in_dim(a_tiles, begin, FR_DEV, 0)
        column_block = lax.dynamic_slice_in_dim(columns, begin, FR_DEV, 0)
        offset_block = lax.dynamic_slice_in_dim(offsets_all, begin, FR_DEV, 0)
        inverse_block = lax.dynamic_slice_in_dim(inverse_diag, begin, FR_DEV, 0)
        tentative_block = lax.dynamic_slice_in_dim(tentative, begin, FR_DEV, 0)
        picked = jnp.take(tentative, column_block, axis=0)[:, :, None]
        coarse_step = neighbour_sum(a_block, picked, offset_block).astype(jnp.bfloat16)
        correction = jnp.einsum("iab,iobc->ioac", inverse_block.astype(jnp.float32), coarse_step.astype(jnp.float32), precision=lax.Precision.HIGHEST)
        return (tentative_block.astype(jnp.float32)[:, None] * centre - OMEGA * correction).astype(jnp.bfloat16)

    smooth = lax.map(smooth_block, jnp.arange(blocks, dtype=jnp.int32)).reshape(total_rows, 3, tile_order, tile_order)

    def assemble(coarse, index):
        begin = (index * FR_DEV).astype(jnp.int32)
        a_block = lax.dynamic_slice_in_dim(a_tiles, begin, FR_DEV, 0)
        column_block = lax.dynamic_slice_in_dim(columns, begin, FR_DEV, 0)
        offset_block = lax.dynamic_slice_in_dim(offsets_all, begin, FR_DEV, 0)
        aggregate_block = lax.dynamic_slice_in_dim(aggregate, begin, FR_DEV, 0)
        smooth_rows = lax.dynamic_slice_in_dim(smooth, begin, FR_DEV, 0)
        picked = jnp.take(smooth, column_block, axis=0)
        product = neighbour_sum(a_block, picked, offset_block).astype(jnp.bfloat16)
        window = window_sum(smooth_rows, product, aggregate_block - aggregate_block[0], WIN)
        first = aggregate_block[0].astype(jnp.int32)
        current = lax.dynamic_slice_in_dim(coarse, first, WIN, 0)
        return lax.dynamic_update_slice_in_dim(coarse, current + window, first, 0), None

    coarse = jnp.zeros((NC + WIN + 1, 7, tile_order, tile_order), jnp.float32)
    coarse, unused = lax.scan(assemble, coarse, jnp.arange(blocks, dtype=jnp.int32))
    return coarse[1:NC + 1]
```

```python
import functools

import jax
import jax.numpy as jnp
from jax import lax
from jax.experimental import pallas as pl
from jax.experimental.pallas import tpu as pltpu
from jax.sharding import PartitionSpec as P

OMEGA = 0.6
ROWS = 16
K = 4
B = 128
AGG_MAX = 3
BANDS = 7
EDGE = 5

ANY = pl.BlockSpec(memory_space=pl.ANY)
SMEM = pl.BlockSpec(memory_space=pltpu.SMEM)
VMEM = pl.BlockSpec(memory_space=pltpu.VMEM)
DMA = pltpu.SemaphoreType.DMA
BF16 = jnp.bfloat16
F32 = jnp.float32


def params(mib):
    return pltpu.CompilerParams(vmem_limit_bytes=mib << 20)


def dot(x, y):
    return jnp.dot(x, y, preferred_element_type=F32)


def fetch(sem, pairs):
    copies = [pltpu.make_async_copy(src, dst, sem.at[n]) for n, (src, dst) in enumerate(pairs)]
    for copy in copies:
        copy.start()
    for copy in copies:
        copy.wait()


def place(columns, aggregate, i, k):
    local = columns[i, k] - columns[0, 0]
    inside = jnp.clip(local, 0, ROWS - 1)
    near = aggregate[inside] - aggregate[i]
    offset = jnp.where(local < 0, -1, jnp.where(local >= ROWS, 1, near))
    return local, offset


def centre_kernel(columns, aggregate, a, t_hbm, inv, s1, t, sem):
    t[ROWS] = jnp.zeros((B, B), BF16)
    fetch(sem, [(t_hbm, t.at[pl.ds(0, ROWS)])])

    def step(i, carry):
        picks = []
        for k in range(K):
            local, offset = place(columns, aggregate, i, k)
            picks.append(t[jnp.where(offset == 0, jnp.clip(local, 0, ROWS - 1), ROWS)])
        wide = jnp.concatenate([a[i, k] for k in range(K)], axis=1)
        stepped = dot(wide, jnp.concatenate(picks, axis=0)).astype(BF16)
        s1[i] = (t[i].astype(F32) - OMEGA * dot(inv[i], stepped)).astype(BF16)
        return carry

    lax.fori_loop(0, ROWS, step, 0, unroll=2)


def sides_kernel(columns, aggregate, a, t_hbm, left_hbm, right_hbm, inv, s0, s2, t, sem):
    zero = 3 * ROWS
    t[zero] = jnp.zeros((B, B), BF16)
    fetch(
        sem,
        [
            (left_hbm, t.at[pl.ds(0, ROWS)]),
            (t_hbm, t.at[pl.ds(ROWS, ROWS)]),
            (right_hbm, t.at[pl.ds(2 * ROWS, ROWS)]),
        ],
    )

    def step(i, carry):
        picks = []
        for k in range(1, K):
            local, offset = place(columns, aggregate, i, k)
            at = jnp.clip(local + ROWS, 0, 3 * ROWS - 1)
            low = t[jnp.where(offset == -1, at, zero)]
            high = t[jnp.where(offset == 1, at, zero)]
            picks.append(jnp.concatenate([low, high], axis=1))
        wide = jnp.concatenate([a[i, k] for k in range(1, K)], axis=1)
        stepped = dot(wide, jnp.concatenate(picks, axis=0)).astype(BF16)
        moved = (-OMEGA * dot(inv[i], stepped)).astype(BF16)
        s0[i] = moved[:, :B]
        s2[i] = moved[:, B:]
        return carry

    lax.fori_loop(0, ROWS, step, 0, unroll=2)


def inner_kernel(columns, aggregate, a, s0_hbm, s1_hbm, s2_hbm, x, v, s, total, sem):
    zero = 3 * ROWS
    s[zero] = jnp.zeros((B, B), BF16)
    x[...] = jnp.zeros_like(x)
    total[...] = jnp.zeros_like(total)
    parts = (s0_hbm, s1_hbm, s2_hbm)
    fetch(sem, [(part, s.at[pl.ds(o * ROWS, ROWS)]) for o, part in enumerate(parts)])

    def step(i, carry):
        turned = jnp.concatenate([s[o * ROWS + i].T for o in range(3)], axis=0)
        rows = []
        for k in range(K):
            local, offset = place(columns, aggregate, i, k)
            here = (local >= 0) & (local < ROWS)
            tiles = []
            for q in range(5):
                o = q - offset - 1
                use = here & (o >= 0) & (o < 3)
                tiles.append(s[jnp.where(use, o * ROWS + local, zero)])
            rows.append(jnp.concatenate(tiles, axis=1))
            if k > 0:
                at = jnp.clip(jnp.where(local < 0, local + ROWS, local), 0, 2 * ROWS - 1)

                @pl.when(jnp.logical_not(here))
                def _(at=at, k=k):
                    total[at] += dot(turned, a[i, k])

        wide = jnp.concatenate([a[i, k] for k in range(K)], axis=1)
        product = dot(wide, jnp.concatenate(rows, axis=0)).astype(BF16)
        part = dot(turned, product)
        group = aggregate[i] - aggregate[0]
        for o in range(3):
            for q in range(5):
                x[group + o, q - o + 2] += part[o * B : (o + 1) * B, q * B : (q + 1) * B]
        return carry

    lax.fori_loop(0, ROWS, step, 0)
    v[...] = total[...].astype(BF16)


def crossing(v, side, picks):
    wide = jnp.concatenate([v[side * ROWS + j] for j in range(ROWS)], axis=1)
    high = jnp.concatenate([jnp.concatenate([part[j] for part in picks], axis=1) for j in range(ROWS)], axis=0)
    return dot(wide, high)


def middle_kernel(v, l1, r1, y):
    for side, part in enumerate((l1, r1)):
        y[side] = crossing(v, side, [part])


def outer_kernel(aggregate, x, v, y, l0, l2, r0, r2, rim_low, rim_high, mine, whole):
    whole[...] = x[...]
    last = aggregate[ROWS - 1] - aggregate[0]
    for side, halos in enumerate(((l0, l2), (r0, r2))):
        part = crossing(v, side, halos)
        for o in range(3):
            row = slice(o * B, (o + 1) * B)
            for p, tile in enumerate((part[row, :B], y[side, row, :], part[row, B:])):
                if side == 0:
                    whole[o, p - o + 2] += tile
                else:
                    whole[last + o, p - o + 4] += tile
    rim_low[...] = whole[0, 2:].astype(BF16)
    rim_high[...] = whole[last + 2, :EDGE].astype(BF16)
    mine[...] = whole[1 : 1 + AGG_MAX]


def slice_kernel(aggregate, me, own, low, high, *rest):
    sends, mine = rest[:-1], rest[-1]
    mine[...] = own[...]
    last = aggregate[ROWS - 1] - aggregate[0]
    mine[0, :EDGE] += low[...].astype(F32)
    mine[last, BANDS - EDGE :] += high[...].astype(F32)
    count = len(sends)
    depth = B // count
    for n, send in enumerate(sends):
        begin = pl.multiple_of(lax.rem(me[0] + n, count) * depth, depth)
        for r in range(AGG_MAX):
            send[r] = mine[r, :, pl.ds(begin, depth), :].astype(BF16)


def gather_kernel(firsts, me, *rest):
    parts, out = rest[:-1], rest[-1]
    count = len(parts)
    rows = out.shape[0]
    for n, part in enumerate(parts):
        source = lax.rem(me[0] + count - n, count)
        begin = firsts[source] - firsts[0]
        after = jnp.where(source == count - 1, rows, firsts[jnp.minimum(source + 1, count - 1)] - firsts[0])
        for r in range(AGG_MAX):

            @pl.when(begin + r < after)
            def _(part=part, r=r, begin=begin):
                out[begin + r] = part[r].astype(F32)


def tiles(*lead, dtype=BF16):
    return jax.ShapeDtypeStruct((*lead, B, B), dtype)


def cost(products, size):
    return pl.CostEstimate(flops=2 * products * B**3, bytes_accessed=size, transcendentals=0)


def both_ways(cells):
    axes = ("dom", "sub")
    count = lax.axis_size(axes)
    up = lax.ppermute(cells, axes, [(n, n + 1) for n in range(count - 1)])
    down = lax.ppermute(cells, axes, [(n + 1, n) for n in range(count - 1)])
    return up, down


def swap(to_next, to_previous):
    axes = ("dom", "sub")
    count = lax.axis_size(axes)
    from_previous = lax.ppermute(to_next, axes, [(n, n + 1) for n in range(count - 1)])
    from_next = lax.ppermute(to_previous, axes, [(n + 1, n) for n in range(count - 1)])
    return from_previous, from_next


def shards(a_tiles, columns, aggregate, tentative, inverse_diag):
    count = lax.axis_size("sub")
    me = lax.axis_index("sub").astype(jnp.int32).reshape(1)
    firsts = lax.all_gather(aggregate[:1], "sub", axis=0, tiled=True)

    t_left, t_right = both_ways(tentative)
    s1 = pl.pallas_call(
        centre_kernel,
        out_shape=tiles(ROWS),
        in_specs=[SMEM, SMEM, VMEM, ANY, VMEM],
        out_specs=VMEM,
        scratch_shapes=[pltpu.VMEM((ROWS + 1, B, B), BF16), DMA((1,))],
        compiler_params=params(16),
        cost_estimate=cost(80, 4 << 20),
    )(columns, aggregate, a_tiles, tentative, inverse_diag)
    l1, r1 = both_ways(s1)
    t_left, t_right, _, firsts = lax.optimization_barrier((t_left, t_right, s1, firsts))
    s0, s2 = pl.pallas_call(
        sides_kernel,
        out_shape=(tiles(ROWS), tiles(ROWS)),
        in_specs=[SMEM, SMEM, VMEM, ANY, ANY, ANY, VMEM],
        out_specs=(VMEM, VMEM),
        scratch_shapes=[pltpu.VMEM((3 * ROWS + 1, B, B), BF16), DMA((3,))],
        compiler_params=params(16),
        cost_estimate=cost(128, 5 << 20),
    )(columns, aggregate, a_tiles, tentative, t_left, t_right, inverse_diag)
    l2, r0 = swap(s2, s0)
    l0, r2 = swap(s0, s2)
    x, v = pl.pallas_call(
        inner_kernel,
        out_shape=(tiles(AGG_MAX + 2, BANDS, dtype=F32), jax.ShapeDtypeStruct((2 * ROWS, 3 * B, B), BF16)),
        in_specs=[SMEM, SMEM, VMEM, ANY, ANY, ANY],
        out_specs=(VMEM, VMEM),
        scratch_shapes=[
            pltpu.VMEM((3 * ROWS + 1, B, B), BF16),
            pltpu.VMEM((2 * ROWS, 3 * B, B), F32),
            DMA((3,)),
        ],
        compiler_params=params(24),
        cost_estimate=cost(1, 1 << 10),
    )(columns, aggregate, a_tiles, s0, s1, s2)
    y = pl.pallas_call(
        middle_kernel,
        out_shape=jax.ShapeDtypeStruct((2, 3 * B, B), F32),
        in_specs=[VMEM] * 3,
        out_specs=VMEM,
        compiler_params=params(16),
        cost_estimate=cost(1, 1 << 10),
    )(v, l1, r1)
    rim_low, rim_high, mine = pl.pallas_call(
        outer_kernel,
        out_shape=(tiles(EDGE), tiles(EDGE), tiles(AGG_MAX, BANDS, dtype=F32)),
        in_specs=[SMEM] + [VMEM] * 7,
        out_specs=(VMEM, VMEM, VMEM),
        scratch_shapes=[pltpu.VMEM((AGG_MAX + 2, BANDS, B, B), F32)],
        compiler_params=params(24),
        cost_estimate=cost(288, 9 << 20),
    )(aggregate, x, v, y, l0, l2, r0, r2)
    low, high = swap(rim_high, rim_low)
    depth = B // count
    piece = jax.ShapeDtypeStruct((AGG_MAX, BANDS, depth, B), BF16)
    sends = pl.pallas_call(
        slice_kernel,
        out_shape=(piece,) * count,
        in_specs=[SMEM, SMEM, VMEM, VMEM, VMEM],
        out_specs=(VMEM,) * count,
        scratch_shapes=[pltpu.VMEM((AGG_MAX, BANDS, B, B), F32)],
        compiler_params=params(16),
        cost_estimate=cost(1, 3 << 20),
    )(aggregate, me, mine, low, high)
    parts = [sends[0]]
    for n in range(1, count):
        parts.append(lax.ppermute(sends[n], "sub", [(i, (i + n) % count) for i in range(count)]))
    rows = lax.axis_size("sub") * 2
    return pl.pallas_call(
        gather_kernel,
        out_shape=jax.ShapeDtypeStruct((rows, BANDS, depth, B), F32),
        in_specs=[SMEM, SMEM] + [VMEM] * count,
        out_specs=VMEM,
        compiler_params=params(16),
        cost_estimate=cost(1, 2 << 20),
    )(firsts, me, *parts)


def solution(mesh):
    return jax.shard_map(
        shards,
        mesh=mesh,
        in_specs=(
            P(("dom", "sub"), None, None, None),
            P(("dom", "sub"), None),
            P(("dom", "sub")),
            P(("dom", "sub"), None, None),
            P(("dom", "sub"), None, None),
        ),
        out_specs=P("dom", None, "sub", None),
        check_vma=False,
    )
```

```python
import functools

import jax
import jax.numpy as jnp
from jax import lax
from jax.experimental import pallas as pl
from jax.experimental.pallas import tpu as pltpu
from jax.sharding import PartitionSpec as P

OMEGA = 0.6
ROWS = 16
K = 4
B = 128
AGG_MAX = 3
BANDS = 7
EDGE = 5

ANY = pl.BlockSpec(memory_space=pl.ANY)
SMEM = pl.BlockSpec(memory_space=pltpu.SMEM)
VMEM = pl.BlockSpec(memory_space=pltpu.VMEM)
DMA = pltpu.SemaphoreType.DMA
BF16 = jnp.bfloat16
F32 = jnp.float32


def params(mib):
    return pltpu.CompilerParams(vmem_limit_bytes=mib << 20)


def dot(x, y):
    return jnp.dot(x, y, preferred_element_type=F32)


def fetch(sem, pairs):
    copies = [pltpu.make_async_copy(src, dst, sem.at[n]) for n, (src, dst) in enumerate(pairs)]
    for copy in copies:
        copy.start()
    for copy in copies:
        copy.wait()


def place(columns, aggregate, i, k):
    local = columns[i, k] - columns[0, 0]
    inside = jnp.clip(local, 0, ROWS - 1)
    near = aggregate[inside] - aggregate[i]
    offset = jnp.where(local < 0, -1, jnp.where(local >= ROWS, 1, near))
    return local, offset


def centre_kernel(columns, aggregate, a, t_hbm, inv, s1, t, sem):
    t[ROWS] = jnp.zeros((B, B), BF16)
    fetch(sem, [(t_hbm, t.at[pl.ds(0, ROWS)])])

    def step(i, carry):
        picks = []
        for k in range(K):
            local, offset = place(columns, aggregate, i, k)
            picks.append(t[jnp.where(offset == 0, jnp.clip(local, 0, ROWS - 1), ROWS)])
        wide = jnp.concatenate([a[i, k] for k in range(K)], axis=1)
        stepped = dot(wide, jnp.concatenate(picks, axis=0)).astype(BF16)
        s1[i] = (t[i].astype(F32) - OMEGA * dot(inv[i], stepped)).astype(BF16)
        return carry

    lax.fori_loop(0, ROWS, step, 0, unroll=2)


def sides_kernel(columns, aggregate, a, t_hbm, left_hbm, right_hbm, inv, s0, s2, t, sem):
    zero = 3 * ROWS
    t[zero] = jnp.zeros((B, B), BF16)
    fetch(
        sem,
        [
            (left_hbm, t.at[pl.ds(0, ROWS)]),
            (t_hbm, t.at[pl.ds(ROWS, ROWS)]),
            (right_hbm, t.at[pl.ds(2 * ROWS, ROWS)]),
        ],
    )

    def step(i, carry):
        picks = []
        for k in range(1, K):
            local, offset = place(columns, aggregate, i, k)
            at = jnp.clip(local + ROWS, 0, 3 * ROWS - 1)
            low = t[jnp.where(offset == -1, at, zero)]
            high = t[jnp.where(offset == 1, at, zero)]
            picks.append(jnp.concatenate([low, high], axis=1))
        wide = jnp.concatenate([a[i, k] for k in range(1, K)], axis=1)
        stepped = dot(wide, jnp.concatenate(picks, axis=0)).astype(BF16)
        moved = (-OMEGA * dot(inv[i], stepped)).astype(BF16)
        s0[i] = moved[:, :B]
        s2[i] = moved[:, B:]
        return carry

    lax.fori_loop(0, ROWS, step, 0, unroll=2)


def inner_kernel(columns, aggregate, a, s0_hbm, s1_hbm, s2_hbm, x, v, s, total, sem):
    zero = 3 * ROWS
    s[zero] = jnp.zeros((B, B), BF16)
    x[...] = jnp.zeros_like(x)
    total[...] = jnp.zeros_like(total)
    parts = (s0_hbm, s1_hbm, s2_hbm)
    fetch(sem, [(part, s.at[pl.ds(o * ROWS, ROWS)]) for o, part in enumerate(parts)])

    def step(i, carry):
        turned = jnp.concatenate([s[o * ROWS + i].T for o in range(3)], axis=0)
        rows = []
        for k in range(K):
            local, offset = place(columns, aggregate, i, k)
            here = (local >= 0) & (local < ROWS)
            tiles = []
            for q in range(5):
                o = q - offset - 1
                use = here & (o >= 0) & (o < 3)
                tiles.append(s[jnp.where(use, o * ROWS + local, zero)])
            rows.append(jnp.concatenate(tiles, axis=1))
            if k > 0:
                at = jnp.clip(jnp.where(local < 0, local + ROWS, local), 0, 2 * ROWS - 1)

                @pl.when(jnp.logical_not(here))
                def _(at=at, k=k):
                    total[at] += dot(turned, a[i, k])

        wide = jnp.concatenate([a[i, k] for k in range(K)], axis=1)
        product = dot(wide, jnp.concatenate(rows, axis=0)).astype(BF16)
        part = dot(turned, product)
        group = aggregate[i] - aggregate[0]
        for o in range(3):
            for q in range(5):
                x[group + o, q - o + 2] += part[o * B : (o + 1) * B, q * B : (q + 1) * B]
        return carry

    lax.fori_loop(0, ROWS, step, 0)
    v[...] = total[...].astype(BF16)


def crossing(v, side, picks):
    wide = jnp.concatenate([v[side * ROWS + j] for j in range(ROWS)], axis=1)
    high = jnp.concatenate([jnp.concatenate([part[j] for part in picks], axis=1) for j in range(ROWS)], axis=0)
    return dot(wide, high)


def middle_kernel(v, l1, r1, y):
    for side, part in enumerate((l1, r1)):
        y[side] = crossing(v, side, [part])


def outer_kernel(aggregate, x, v, y, l0, l2, r0, r2, rim_low, rim_high, mine, whole):
    whole[...] = x[...]
    last = aggregate[ROWS - 1] - aggregate[0]
    for side, halos in enumerate(((l0, l2), (r0, r2))):
        part = crossing(v, side, halos)
        for o in range(3):
            row = slice(o * B, (o + 1) * B)
            for p, tile in enumerate((part[row, :B], y[side, row, :], part[row, B:])):
                if side == 0:
                    whole[o, p - o + 2] += tile
                else:
                    whole[last + o, p - o + 4] += tile
    rim_low[...] = whole[0, 2:].astype(BF16)
    rim_high[...] = whole[last + 2, :EDGE].astype(BF16)
    mine[...] = whole[1 : 1 + AGG_MAX]


def slice_kernel(aggregate, me, base, own, low, high, *rest):
    sends, mine = rest[:-1], rest[-1]
    mine[...] = own[...]
    last = aggregate[ROWS - 1] - aggregate[0]
    mine[0, :EDGE] += low[...].astype(F32)
    mine[last, BANDS - EDGE :] += high[...].astype(F32)
    count = len(sends)
    depth = B // count
    first = jnp.full((depth, B), (aggregate[0] - base[0]).astype(F32), F32).astype(BF16)
    for n, send in enumerate(sends):
        begin = pl.multiple_of(lax.rem(me[0] + n, count) * depth, depth)
        for r in range(AGG_MAX):
            send[r * BANDS : (r + 1) * BANDS] = mine[r, :, pl.ds(begin, depth), :].astype(BF16)
        send[AGG_MAX * BANDS] = first


def gather_kernel(me, *rest):
    parts, out, firsts = rest[:-2], rest[-2], rest[-1]
    count = len(parts)
    rows = out.shape[0]
    firsts[count] = rows
    for n, part in enumerate(parts):
        firsts[lax.rem(me[0] + count - n, count)] = jnp.max(part[AGG_MAX * BANDS].astype(F32)).astype(jnp.int32)
    for n, part in enumerate(parts):
        source = lax.rem(me[0] + count - n, count)
        begin = firsts[source]
        after = firsts[source + 1]
        for r in range(AGG_MAX):

            @pl.when(begin + r < after)
            def _(part=part, r=r, begin=begin):
                out[begin + r] = part[r * BANDS : (r + 1) * BANDS].astype(F32)


def tiles(*lead, dtype=BF16):
    return jax.ShapeDtypeStruct((*lead, B, B), dtype)


def cost(products, size):
    return pl.CostEstimate(flops=2 * products * B**3, bytes_accessed=size, transcendentals=0)


def both_ways(cells):
    axes = ("dom", "sub")
    count = lax.axis_size(axes)
    up = lax.ppermute(cells, axes, [(n, n + 1) for n in range(count - 1)])
    down = lax.ppermute(cells, axes, [(n + 1, n) for n in range(count - 1)])
    return up, down


def swap(to_next, to_previous):
    axes = ("dom", "sub")
    count = lax.axis_size(axes)
    from_previous = lax.ppermute(to_next, axes, [(n, n + 1) for n in range(count - 1)])
    from_next = lax.ppermute(to_previous, axes, [(n + 1, n) for n in range(count - 1)])
    return from_previous, from_next


def shards(a_tiles, columns, aggregate, tentative, inverse_diag):
    count = lax.axis_size("sub")
    me = lax.axis_index("sub").astype(jnp.int32).reshape(1)
    base = lax.axis_index("dom").astype(jnp.int32).reshape(1) * (2 * count)

    t_left, t_right = both_ways(tentative)
    s1 = pl.pallas_call(
        centre_kernel,
        out_shape=tiles(ROWS),
        in_specs=[SMEM, SMEM, VMEM, ANY, VMEM],
        out_specs=VMEM,
        scratch_shapes=[pltpu.VMEM((ROWS + 1, B, B), BF16), DMA((1,))],
        compiler_params=params(16),
        cost_estimate=cost(80, 4 << 20),
    )(columns, aggregate, a_tiles, tentative, inverse_diag)
    l1, r1 = both_ways(s1)
    t_left, t_right, _ = lax.optimization_barrier((t_left, t_right, s1))
    s0, s2 = pl.pallas_call(
        sides_kernel,
        out_shape=(tiles(ROWS), tiles(ROWS)),
        in_specs=[SMEM, SMEM, VMEM, ANY, ANY, ANY, VMEM],
        out_specs=(VMEM, VMEM),
        scratch_shapes=[pltpu.VMEM((3 * ROWS + 1, B, B), BF16), DMA((3,))],
        compiler_params=params(16),
        cost_estimate=cost(128, 5 << 20),
    )(columns, aggregate, a_tiles, tentative, t_left, t_right, inverse_diag)
    l2, r0 = swap(s2, s0)
    l0, r2 = swap(s0, s2)
    x, v = pl.pallas_call(
        inner_kernel,
        out_shape=(tiles(AGG_MAX + 2, BANDS, dtype=F32), jax.ShapeDtypeStruct((2 * ROWS, 3 * B, B), BF16)),
        in_specs=[SMEM, SMEM, VMEM, ANY, ANY, ANY],
        out_specs=(VMEM, VMEM),
        scratch_shapes=[
            pltpu.VMEM((3 * ROWS + 1, B, B), BF16),
            pltpu.VMEM((2 * ROWS, 3 * B, B), F32),
            DMA((3,)),
        ],
        compiler_params=params(24),
        cost_estimate=cost(1, 1 << 10),
    )(columns, aggregate, a_tiles, s0, s1, s2)
    y = pl.pallas_call(
        middle_kernel,
        out_shape=jax.ShapeDtypeStruct((2, 3 * B, B), F32),
        in_specs=[VMEM] * 3,
        out_specs=VMEM,
        compiler_params=params(16),
        cost_estimate=cost(1, 1 << 10),
    )(v, l1, r1)
    rim_low, rim_high, mine = pl.pallas_call(
        outer_kernel,
        out_shape=(tiles(EDGE), tiles(EDGE), tiles(AGG_MAX, BANDS, dtype=F32)),
        in_specs=[SMEM] + [VMEM] * 7,
        out_specs=(VMEM, VMEM, VMEM),
        scratch_shapes=[pltpu.VMEM((AGG_MAX + 2, BANDS, B, B), F32)],
        compiler_params=params(24),
        cost_estimate=cost(288, 9 << 20),
    )(aggregate, x, v, y, l0, l2, r0, r2)
    low, high = swap(rim_high, rim_low)
    depth = B // count
    piece = jax.ShapeDtypeStruct((AGG_MAX * BANDS + 1, depth, B), BF16)
    sends = pl.pallas_call(
        slice_kernel,
        out_shape=(piece,) * count,
        in_specs=[SMEM, SMEM, SMEM, VMEM, VMEM, VMEM],
        out_specs=(VMEM,) * count,
        scratch_shapes=[pltpu.VMEM((AGG_MAX, BANDS, B, B), F32)],
        compiler_params=params(16),
        cost_estimate=cost(1, 3 << 20),
    )(aggregate, me, base, mine, low, high)
    parts = [sends[0]]
    for n in range(1, count):
        parts.append(lax.ppermute(sends[n], "sub", [(i, (i + n) % count) for i in range(count)]))
    rows = lax.axis_size("sub") * 2
    return pl.pallas_call(
        gather_kernel,
        out_shape=jax.ShapeDtypeStruct((rows, BANDS, depth, B), F32),
        in_specs=[SMEM] + [VMEM] * count,
        out_specs=VMEM,
        scratch_shapes=[pltpu.SMEM((count + 1,), jnp.int32)],
        compiler_params=params(16),
        cost_estimate=cost(1, 2 << 20),
    )(me, *parts)


def solution(mesh):
    return jax.shard_map(
        shards,
        mesh=mesh,
        in_specs=(
            P(("dom", "sub"), None, None, None),
            P(("dom", "sub"), None),
            P(("dom", "sub")),
            P(("dom", "sub"), None, None),
            P(("dom", "sub"), None, None),
        ),
        out_specs=P("dom", None, "sub", None),
        check_vma=False,
    )
```
